32 devices in a mesh: groups: 2 (over y), ep: 8 (over z, x), tp: 2 (over core).
Axes of the slice: x: 2, y: 2, z: 4, core: 2. Of those that a mesh axis runs over, the one named last changes fastest.
Arguments:
- residual: bfloat16 [256, 1440], P(('groups', 'ep')), parts along dimension 0, may hold values from -6 to 6
- queries: bfloat16 [256, 2048], P(('groups', 'ep'), 'tp'), parts along dimension 0, may hold values from -7 to 7
- new_kv: bfloat16 [256, 2, 512], P(('groups', 'ep'), None, 'tp'), parts along dimension 0, may hold values from -6 to 6
- kv_cache: bfloat16 [256, 2, 8, 64, 256], P(('groups', 'ep'), None, 'tp'), parts along dimension 0, may hold values from -7 to 7
- cache_len: int32 [256], P(('groups', 'ep')), parts along dimension 0, may hold values from 2 to 255, as said below
- move_slot: int32 [32], P(('groups', 'ep')), parts along dimension 0, may hold values from 0 to 15, as said below
- move_dest: int32 [32], P(('groups', 'ep')), parts along dimension 0, may hold values from 0 to 7, as said below
- sink_logits: float32 [32], P('tp'), may hold values from -1 to 3
- out_weight: bfloat16 [2048, 1440], P('tp'), may hold values from -0.125 to 0.125
- norm_gain: float32 [1440], replicated, may hold values from 0.1 to 1.9
- router_weight: bfloat16 [1440, 8], replicated, may hold values from -0.3125 to 0.3125
- expert_ids: int32 [256, 4], P(('groups', 'ep')), parts along dimension 0, may hold values from 0 to 7, all different within a row; in each aligned block of 16 rows (0 to 15, 16 to 31, ...) at most 16 rows name the same one
- gate_up: bfloat16 [8, 1440, 2, 1440], P('ep', None, None, 'tp'), may hold values from -0.15625 to 0.15625
- down_weight: bfloat16 [8, 1440, 1440], P('ep', 'tp'), may hold values from -0.15625 to 0.15625
Outputs:
- layer_out: bfloat16 [256, 1440], P(('groups', 'ep'), 'tp'), parts along dimension 0
- cache_out: bfloat16 [256, 2, 8, 64, 256], P(('groups', 'ep'), None, 'tp'), parts along dimension 0
The draws below stay inside these ranges and needn't reach their ends.
There are 2 independent parts, one for each index of `groups`. The reference program is written for one: setup_inputs(seed, part) draws one part's arguments, and reference() takes and returns one part's arrays. A program takes and returns all parts, laid end to end along the dimension named above; an argument that names none is the same for every part. Nothing has to cross between parts.
Inputs may be any that keep to these rules, and one draw needn't show every extreme that they name: `cache_len`: values at most 255, which some row reaches. `move_slot`: the 2 entries of one shard are distinct local rows: those of its rows with the largest cache_len. `move_dest`: for each j, the destinations of entry j over all shards form a permutation of the shards (a shard may keep its row). `expert_ids`: each row names 4 different experts; among the 16 rows of one ep index (new placement) no expert is named by more than 16 rows, a bound that some block reaches.
All inputs are finite; a program needn't handle non-finite values.
Results may differ from the reference program's by a relative error of at most 0.0056.
Values may be sent and summed in bfloat16 or wider, within the bound.
A program may use at most 64 MiB of HBM per device.

```python
import math
import jax
import jax.numpy as jnp
import numpy as np
from jax import lax

D = 1440
FF = 1440
Q_HEADS = 32
KV_HEADS = 8
HD = 64
TOP = 4
R_DEV = 16
CACHE_LEN = 256
MOVES = 2
ROWS = 128
EXPERTS = 8
CAP = 16
MOVE_ALL = 16


def row_lengths(key):
    shard_count = ROWS // R_DEV
    first_key, second_key, third_key = jax.random.split(key, 3)
    ceiling = jax.random.randint(first_key, (shard_count, 1), CACHE_LEN // 4, CACHE_LEN)
    spread = jax.random.randint(second_key, (shard_count, R_DEV), 0, CACHE_LEN)
    lengths = (2 + spread % (ceiling - 2)).reshape(-1)
    longest = jax.random.randint(third_key, (), 0, ROWS)
    return jnp.where(jnp.arange(ROWS) == longest, CACHE_LEN - 1, lengths).astype(jnp.int32)


def draw_cache_len(key, part):
    return row_lengths(key)


def draw_move_slot(key, part):
    lengths = row_lengths(key)
    key = jax.random.fold_in(key, 5)
    tiebreak = jax.random.permutation(key, ROWS).astype(jnp.int32)
    length_score = lengths * ROWS + tiebreak
    chosen = lax.top_k(length_score.reshape(ROWS // R_DEV, R_DEV), MOVES)[1]
    return chosen.reshape(-1).astype(jnp.int32)


def draw_move_dest(key, part):
    key = jax.random.fold_in(key, 7)
    shard_count = ROWS // R_DEV
    columns = [jax.random.permutation(jax.random.fold_in(key, column_index), shard_count) for column_index in range(MOVES)]
    return jnp.stack(columns, axis=1).reshape(-1).astype(jnp.int32)


def draw_kv_cache(key, part):
    key = jax.random.fold_in(key, 3)
    full_shape = (ROWS, 2, KV_HEADS, HD, CACHE_LEN)
    cache_values = jnp.clip(jax.random.normal(key, full_shape, jnp.float32), -6.0, 6.0)
    return cache_values.astype(jnp.bfloat16)


def draw_queries(key, part):
    key = jax.random.fold_in(key, 4)
    full_shape = (ROWS, KV_HEADS, Q_HEADS // KV_HEADS, HD)
    values = jnp.clip(jax.random.normal(key, full_shape, jnp.float32), -6.0, 6.0)
    return values.reshape(ROWS, Q_HEADS * HD).astype(jnp.bfloat16)


def steps_of(key, shape, pieces, low, high):
    def one(position, shards_of):
        heights = jax.random.uniform(jax.random.fold_in(jax.random.fold_in(key, 6), position), (shards_of,), jnp.float32, low / len(pieces), high / len(pieces))
        return jnp.repeat(jnp.exp(heights), shape[position] // shards_of).reshape((-1,) + (1,) * (len(shape) - position - 1))

    factor_of = one(*pieces[0])
    for cut in pieces[1:]:
        factor_of = factor_of * one(*cut)
    return factor_of


def shared_out(own_key, own, number, rows, count, top, limit, skew):
    sequence = jax.random.permutation(own_key, count)
    crowded, ordinary = portions_of(count, rows * top, limit, skew, True), portions_of(count, rows * top, limit, skew, False)
    places = jnp.arange(count)

    def named(sizes, offset_by):
        used = int((sizes > 0).sum())
        fixed = max(1, used // 4)
        passed = fixed + (places - fixed + offset_by * (used - fixed)) % max(1, count - fixed)
        return jnp.zeros((count,), jnp.int32).at[sequence[jnp.where(places < fixed, places, passed)]].set(jnp.asarray(sizes, jnp.int32))

    sizes = jnp.where(number % 4 == 0, named(crowded, number // 4), named(ordinary, number - number // 4 - 1))
    mixed = jax.random.permutation(jax.random.fold_in(own, 3), count)
    source_of, receiver = mixed[0:count // 2 * 2:2], mixed[1:count // 2 * 2:2]
    room = jnp.minimum(sizes[source_of] - 1, limit - sizes[receiver]) // 2
    room = jnp.where((source_of == sequence[0]) | (receiver == sequence[0]) | (sizes[receiver] == 0), 0, jnp.maximum(room, 0))
    passed = jax.random.randint(jax.random.fold_in(own, 4), (count // 2,), 0, 1 << 20) % (room + 1)
    sizes = sizes.at[source_of].add(-passed).at[receiver].add(passed)
    labels = jnp.searchsorted(jnp.cumsum(sizes), jnp.arange(rows * top), side="right").astype(jnp.int32)
    listing = labels.reshape(top, rows).T
    listing = listing[jax.random.permutation(jax.random.fold_in(own, 1), rows)]
    offset_by = jax.random.randint(jax.random.fold_in(own, 2), (rows, 1), 0, top)
    return jnp.take_along_axis(listing, (jnp.arange(top)[None, :] + offset_by) % top, axis=1)


def portions_of(number_of, total, most, slope, full):
    loads = [(1 << 20) // math.isqrt(standing ** slope) + 1 for standing in range(1, number_of + 1)]
    largest = most if full else min(most, max(-(-total // number_of), total * loads[0] // sum(loads)))
    least = 1 if total - largest >= number_of - 1 else 0
    counts, rest = [largest] + [least] * (number_of - 1), total - largest - least * (number_of - 1)
    while rest > 0:
        movable = [i for i in range(1, number_of) if counts[i] < largest] or [i for i in range(1, number_of) if counts[i] < most]
        pool, budget = sum([loads[i] for i in movable]), rest
        for i in movable:
            extra = min(most - counts[i], max(1, budget * loads[i] // pool), rest)
            counts[i] = counts[i] + extra
            rest = rest - extra
    return np.array(counts)


def noise(key, shape, scale, limit, cuts=(), held_as=jnp.bfloat16):
    factor_of = steps_of(key, shape, cuts, -0.22, 0.18) if cuts else 1.0
    result = jax.random.normal(key, shape, jnp.float32) * scale * factor_of
    return jnp.minimum(jnp.maximum(result, -limit), limit).astype(held_as)


def setup_inputs(seed: int = 0, part: int = 0) -> dict:
    key_of = jax.random.split(jax.random.key(seed), 15)
    own_keys = jax.random.split(jax.random.fold_in(key_of[14], part), 15)
    residual = noise(own_keys[0], (ROWS, D), 1.0, 6.0, ((0, 8),))
    queries = draw_queries(jax.random.fold_in(jax.random.fold_in(key_of[14], part), 71), part)
    new_kv = noise(own_keys[2], (ROWS, 2, KV_HEADS * HD), 1.0, 6.0, ((0, 8), (2, 2)))
    kv_cache = draw_kv_cache(jax.random.fold_in(jax.random.fold_in(key_of[14], part), 71), part)
    cache_len = draw_cache_len(jax.random.fold_in(jax.random.fold_in(key_of[14], part), 71), part)
    move_slot = draw_move_slot(jax.random.fold_in(jax.random.fold_in(key_of[14], part), 71), part)
    move_dest = draw_move_dest(jax.random.fold_in(jax.random.fold_in(key_of[14], part), 71), part)
    sink_logits = jnp.clip(-1.0 + 4.0 * jax.random.uniform(key_of[7], (Q_HEADS,), jnp.float32) ** steps_of(key_of[7], (Q_HEADS,), ((0, 2),), -0.2, 0.2), -1.0, 3.0)
    out_weight = noise(key_of[8], (Q_HEADS * HD, D), (Q_HEADS * HD) ** -0.5, 0.125, ((0, 2),))
    norm_gain = jnp.clip(1.0 + 0.18 * jax.random.normal(key_of[9], (D,), jnp.float32), 0.1, 1.9)
    router_weight = noise(key_of[10], (D, EXPERTS), (D // 4) ** -0.5, 0.3125)
    expert_ids_keys = jax.random.split(jax.random.fold_in(own_keys[11], 1), ROWS // R_DEV)
    expert_ids_turns = jax.random.permutation(jax.random.fold_in(own_keys[11], 3), ROWS // R_DEV)
    expert_ids = jax.vmap(lambda own, number: shared_out(jax.random.fold_in(own_keys[11], 2), own, number, R_DEV, EXPERTS, TOP, CAP, 2))(expert_ids_keys, expert_ids_turns).reshape((ROWS, TOP))
    gate_up = noise(key_of[12], (EXPERTS, D, 2, FF), D ** -0.5, 0.15625, ((0, 8), (3, 2)))
    down_weight = noise(key_of[13], (EXPERTS, FF, D), FF ** -0.5, 0.15625, ((0, 8), (1, 2)))
    return dict(residual=residual, queries=queries, new_kv=new_kv, kv_cache=kv_cache, cache_len=cache_len, move_slot=move_slot, move_dest=move_dest, sink_logits=sink_logits, out_weight=out_weight, norm_gain=norm_gain, router_weight=router_weight, expert_ids=expert_ids, gate_up=gate_up, down_weight=down_weight)


ALPHA = 1.702
EPSILON = 1e-05

def insert_token(cache_values, new_rows, lengths):
    row_count = cache_values.shape[0]
    kv_count = cache_values.shape[2]
    head_dim = cache_values.shape[3]
    length = cache_values.shape[4]
    fresh_rows = new_rows.reshape(row_count, 2, kv_count, head_dim, 1)
    position_index = lax.broadcasted_iota(jnp.int32, (row_count, 1, 1, 1, length), 4)
    return jnp.where(position_index == lengths.reshape(row_count, 1, 1, 1, 1), fresh_rows, cache_values)

def attend_rows(queries, cache_values, lengths, sink_logits):
    row_count = cache_values.shape[0]
    kv_count = cache_values.shape[2]
    head_dim = cache_values.shape[3]
    length = cache_values.shape[4]
    group = queries.shape[1] // (kv_count * head_dim)
    query_rows = queries.reshape(row_count, kv_count, group, head_dim).astype(jnp.float32)
    scores = jnp.einsum('rgqd,rgdl->rgql', query_rows, cache_values[:, 0].astype(jnp.float32)) * head_dim ** (-0.5)
    visible = lax.broadcasted_iota(jnp.int32, (row_count, 1, 1, length), 3) <= lengths.reshape(row_count, 1, 1, 1)
    sink_part = sink_logits.reshape(1, kv_count, group, 1)
    peak_score = jnp.maximum(lax.optimization_barrier(jnp.max(jnp.where(visible, scores, -1e+30), axis=3, keepdims=True)), sink_part)
    weights = jnp.where(visible, jnp.exp(scores - peak_score), 0.0)
    total_mass = lax.optimization_barrier(jnp.sum(weights, axis=3, keepdims=True)) + jnp.exp(sink_part - peak_score)
    probabilities = (weights / total_mass).astype(jnp.bfloat16)
    mixture = jnp.einsum('rgql,rgdl->rgqd', probabilities.astype(jnp.float32), cache_values[:, 1].astype(jnp.float32))
    return mixture.astype(jnp.bfloat16).reshape(row_count, -1)

def reference(residual, queries, new_kv, kv_cache, cache_len, move_slot, move_dest, sink_logits, out_weight, norm_gain, router_weight, expert_ids, gate_up, down_weight):
    entry_index = jnp.arange(MOVE_ALL, dtype=jnp.int32)
    column = entry_index % MOVES
    source = entry_index // MOVES * R_DEV + move_slot
    target = move_dest * R_DEV + move_slot[move_dest * MOVES + column]
    anchor = jnp.arange(ROWS, dtype=jnp.int32).at[target].set(source)
    lengths = cache_len[anchor]
    cache_out = insert_token(kv_cache[anchor], new_kv[anchor], lengths)
    heads = attend_rows(queries[anchor], cache_out, lengths, sink_logits)
    stream = residual[anchor].astype(jnp.float32) + jnp.dot(heads, out_weight, preferred_element_type=jnp.float32)
    mean_square = lax.optimization_barrier(jnp.mean(stream * stream, axis=1, keepdims=True))
    normed = stream * lax.rsqrt(mean_square + EPSILON) * norm_gain
    tokens = normed.astype(jnp.bfloat16)
    logits = jnp.dot(normed, router_weight.astype(jnp.float32), precision=lax.Precision.HIGHEST)
    raised = jnp.exp(jnp.take_along_axis(logits, expert_ids, axis=1))
    gate_weights = raised / lax.optimization_barrier(jnp.sum(raised, axis=1, keepdims=True))
    slot_bound = CAP * (ROWS // R_DEV)
    flat_ids = expert_ids.reshape(-1)
    owner_row = jnp.arange(ROWS * TOP, dtype=jnp.int32) // TOP

    def one_expert(expert, collected):
        is_hit = flat_ids == expert
        slot_rank = jnp.cumsum(is_hit.astype(jnp.int32)) - 1
        slot_index = jnp.where(is_hit, slot_rank, slot_bound).astype(jnp.int32)
        chosen = jnp.zeros((slot_bound + 1,), jnp.int32).at[slot_index].set(owner_row)[:slot_bound]
        picked = tokens[chosen]
        gate_and_up = jnp.dot(picked, gate_up[expert].reshape(D, 2 * FF), preferred_element_type=jnp.float32).reshape(slot_bound, 2, FF)
        gate_part = gate_and_up[:, 0]
        up_part = gate_and_up[:, 1]
        hidden = ((up_part + 1.0) * gate_part * jax.nn.sigmoid(ALPHA * gate_part)).astype(jnp.bfloat16)
        expert_out = jnp.dot(hidden, down_weight[expert], preferred_element_type=jnp.float32).astype(jnp.bfloat16)
        padded = jnp.concatenate([expert_out, jnp.zeros((1, D), jnp.bfloat16)], axis=0)
        return jnp.where(is_hit[:, None], padded[slot_index], collected)
    collected = lax.fori_loop(0, EXPERTS, one_expert, jnp.zeros((ROWS * TOP, D), jnp.bfloat16))
    mixture = lax.optimization_barrier(jnp.sum(collected.reshape(ROWS, TOP, D).astype(jnp.float32) * gate_weights[:, :, None], axis=1))
    layer_out = (stream + mixture).astype(jnp.bfloat16)
    return (layer_out, cache_out)
```

```python
import functools

import jax
import jax.numpy as jnp
from jax import lax
from jax.experimental import pallas as pl
from jax.experimental.pallas import tpu as pltpu
from jax.sharding import PartitionSpec as P

ALPHA = 1.702
EPSILON = 1e-05


def insert_token(cache_values, new_rows, lengths):
    row_count = cache_values.shape[0]
    kv_count = cache_values.shape[2]
    head_dim = cache_values.shape[3]
    length = cache_values.shape[4]
    fresh_rows = new_rows.reshape(row_count, 2, kv_count, head_dim, 1)
    position_index = lax.broadcasted_iota(jnp.int32, (row_count, 1, 1, 1, length), 4)
    return jnp.where(
        position_index == lengths.reshape(row_count, 1, 1, 1, 1), fresh_rows, cache_values
    )


def attend_rows(queries, cache_values, lengths, sink_logits):
    row_count = cache_values.shape[0]
    kv_count = cache_values.shape[2]
    head_dim = cache_values.shape[3]
    length = cache_values.shape[4]
    group = queries.shape[1] // (kv_count * head_dim)
    query_rows = queries.reshape(row_count, kv_count, group, head_dim)
    scores = jnp.einsum(
        "rgqd,rgdl->rgql", query_rows, cache_values[:, 0], preferred_element_type=jnp.float32
    ) * head_dim ** (-0.5)
    visible = lax.broadcasted_iota(jnp.int32, (row_count, 1, 1, length), 3) <= lengths.reshape(
        row_count, 1, 1, 1
    )
    sink_part = sink_logits.reshape(1, kv_count, group, 1)
    peak_score = jnp.maximum(
        jnp.max(jnp.where(visible, scores, -1e30), axis=3, keepdims=True), sink_part
    )
    weights = jnp.where(visible, jnp.exp(scores - peak_score), 0.0)
    total_mass = jnp.sum(weights, axis=3, keepdims=True) + jnp.exp(sink_part - peak_score)
    probabilities = (weights / total_mass).astype(jnp.bfloat16)
    mixture = jnp.einsum(
        "rgql,rgdl->rgqd", probabilities, cache_values[:, 1], preferred_element_type=jnp.float32
    )
    return mixture.astype(jnp.bfloat16).reshape(row_count, -1)


def migrate(cache_values, residual, queries, lengths, move_slot, move_dest):
    my_shard = lax.axis_index("ep")
    row_count = residual.shape[0]
    move_count = move_slot.shape[0]
    current = (cache_values, residual, queries, lengths)
    leaving = tuple((jnp.take(member, move_slot, axis=0) for member in current))
    piece = (
        lax.all_gather(leaving[0], "ep", axis=0, tiled=True),
        lax.all_gather(leaving[1], "ep", axis=0, tiled=True),
        lax.all_gather(leaving[2], "ep", axis=0, tiled=True),
        lax.all_gather(leaving[3], "ep", axis=0, tiled=True),
        lax.all_gather(move_dest, "ep", axis=0, tiled=True),
    )
    piece_rows = piece[4].shape[0]
    column = jnp.arange(piece_rows, dtype=jnp.int32) % move_count
    target = jnp.where(piece[4] == my_shard, move_slot[column], row_count)
    return tuple(
        (held.at[target].set(incoming, mode="drop") for held, incoming in zip(current, piece[:4]))
    )


def per_device_general(
    residual,
    queries,
    new_kv,
    kv_cache,
    cache_len,
    move_slot,
    move_dest,
    sink_logits,
    out_weight,
    norm_gain,
    router_weight,
    expert_ids,
    gate_up,
    down_weight,
):
    row_count = residual.shape[0]
    filled = insert_token(kv_cache, new_kv, cache_len)
    cache_new, resid_new, query_new, length_new = migrate(
        filled, residual, queries, cache_len, move_slot, move_dest
    )
    heads = attend_rows(query_new, cache_new, length_new, sink_logits)
    partial_out = jnp.dot(heads, out_weight, preferred_element_type=jnp.float32)
    stream = resid_new.astype(jnp.float32) + lax.psum(partial_out, "tp")
    mean_square = jnp.mean(stream * stream, axis=1, keepdims=True)
    normed = stream * lax.rsqrt(mean_square + EPSILON) * norm_gain
    tokens = normed.astype(jnp.bfloat16)
    logits = jnp.dot(normed, router_weight.astype(jnp.float32), precision=lax.Precision.HIGHEST)
    raised = jnp.exp(jnp.take_along_axis(logits, expert_ids, axis=1))
    gate_weights = raised / jnp.sum(raised, axis=1, keepdims=True)
    top_count = expert_ids.shape[1]
    expert_count = router_weight.shape[1]
    width = tokens.shape[1]
    capacity = max(2, min(row_count, 2 * row_count * top_count // expert_count))
    flat_ids = expert_ids.reshape(-1)
    onehot = (flat_ids[:, None] == jnp.arange(expert_count, dtype=jnp.int32)[None, :]).astype(
        jnp.int32
    )
    slot_rank = jnp.sum((jnp.cumsum(onehot, axis=0) - 1) * onehot, axis=1)
    position = flat_ids * capacity + slot_rank
    owner_row = jnp.arange(row_count * top_count, dtype=jnp.int32) // top_count
    outgoing = (
        jnp.zeros((expert_count * capacity, width), jnp.bfloat16)
        .at[position]
        .set(tokens[owner_row])
    )
    outgoing = outgoing.reshape(expert_count, capacity, width)
    local_experts = gate_up.shape[0]
    share_width = width // lax.axis_size("tp")
    offset = lax.axis_index("tp") * share_width
    features = lax.all_to_all(outgoing, "ep", split_axis=0, concat_axis=0, tiled=True)
    slot_count = features.shape[1]
    grouped = features.reshape(-1, local_experts, slot_count, features.shape[2])
    gate_and_up = jnp.einsum(
        "secd,edkf->seckf", grouped, gate_up, preferred_element_type=jnp.float32
    )
    gate_part = gate_and_up[:, :, :, 0, :]
    up_part = gate_and_up[:, :, :, 1, :]
    hidden = ((up_part + 1.0) * gate_part * jax.nn.sigmoid(ALPHA * gate_part)).astype(jnp.bfloat16)
    partial_down = jnp.einsum(
        "secf,efd->secd", hidden, down_weight, preferred_element_type=jnp.float32
    )
    summed = lax.psum_scatter(
        partial_down.reshape(-1, slot_count, partial_down.shape[3]),
        "tp",
        scatter_dimension=2,
        tiled=True,
    )
    returned = lax.all_to_all(
        summed.astype(jnp.bfloat16), "ep", split_axis=0, concat_axis=0, tiled=True
    )
    back_rows = returned.reshape(expert_count * capacity, -1)[position].astype(jnp.float32)
    mixture = jnp.sum(
        back_rows.reshape(row_count, top_count, -1) * gate_weights[:, :, None], axis=1
    )
    own_stream = lax.dynamic_slice_in_dim(stream, offset, share_width, 1)
    layer_out = (own_stream + mixture).astype(jnp.bfloat16)
    return (layer_out, cache_new)


MESH = pl.DeviceIdType.MESH
F32 = jnp.float32
BF16 = jnp.bfloat16


def wrap(value, size):
    value = jnp.where(value < 0, value + size, value)
    return jnp.where(value >= size, value - size, value)


def step_kernel(
    n_ep,
    n_tp,
    lengths,
    slots,
    meta,
    queries,
    residual,
    sink,
    gain,
    router,
    expert_ids,
    cache_hbm,
    out_hbm,
    gate_up_hbm,
    down_hbm,
    layer_out,
    incoming,
    cache,
    out_w,
    gate_up,
    down_w,
    send1,
    recv1,
    send2,
    recv2,
    meta_all,
    meta_smem,
    mixed,
    heads,
    partial,
    partial_in,
    own_stream,
    streams,
    hidden,
    ysend,
    yrecv,
    local_sem,
    meta_sems,
    one_sems,
    two_sems,
    part_sems,
    stream_sems,
    y_sems,
    in_sem,
):
    ep = lax.axis_index("ep")
    tp = lax.axis_index("tp")
    rows, q_heads, lanes = mixed.shape
    width = residual.shape[1]
    half = width // n_tp
    pieces = cache.shape[1]
    kv = pieces // 2
    hd = cache.shape[2]
    moves = send1.shape[1]
    group = q_heads // kv

    def ahead(k):
        return lax.rem(ep + k, n_ep)

    def behind(k):
        return lax.rem(ep - k + n_ep, n_ep)

    loads = [
        pltpu.make_async_copy(cache_hbm, cache, local_sem.at[0]),
        pltpu.make_async_copy(out_hbm, out_w, local_sem.at[1]),
        pltpu.make_async_copy(gate_up_hbm, gate_up, local_sem.at[2]),
        pltpu.make_async_copy(down_hbm, down_w, local_sem.at[3]),
    ]
    for load in loads:
        load.start()

    barrier = pltpu.get_barrier_semaphore()
    for k in range(n_ep):
        for q in range(n_tp):
            if k or q:
                pl.semaphore_signal(
                    barrier,
                    inc=1,
                    device_id={"ep": ahead(k), "tp": lax.rem(tp + q, n_tp)},
                    device_id_type=MESH,
                )
    pl.semaphore_wait(barrier, n_ep * n_tp - 1)

    def send(src, dst, sems, index, k, q=0):
        target = {"ep": ahead(k)} if k else {}
        if q:
            target["tp"] = lax.rem(tp + q, n_tp)
        copy = pltpu.make_async_remote_copy(
            src_ref=src,
            dst_ref=dst,
            send_sem=sems.at[(0,) + index],
            recv_sem=sems.at[(1,) + index],
            device_id=target,
            device_id_type=MESH,
        )
        copy.start()
        return copy

    meta_copies = [send(meta, meta_all.at[k], meta_sems, (k,), k) for k in range(1, n_ep)]
    meta_all[0] = meta[...]

    loads[0].wait()
    for j in range(moves):
        slot = slots[j]
        for p in range(pieces):
            send1[p, j] = cache[slot, p]
    one_copies = [
        send(send1.at[ahead(k)], recv1.at[k], one_sems, (k,), k) for k in range(1, n_ep)
    ]
    recv1[0] = send1[ep]

    position_index = lax.broadcasted_iota(jnp.int32, (q_heads, cache.shape[3]), 1)
    sink_part = sink[...]

    def attend(r, carry):
        keys = cache[r, 0:kv].reshape(kv * hd, cache.shape[3])
        values = cache[r, kv : 2 * kv].reshape(kv * hd, cache.shape[3])
        scores = jnp.dot(queries[r], keys, preferred_element_type=F32) * hd ** (-0.5)
        visible = position_index <= lengths[r]
        peak = jnp.maximum(
            jnp.max(jnp.where(visible, scores, -1e30), axis=1, keepdims=True), sink_part
        )
        weights = jnp.where(visible, jnp.exp(scores - peak), 0.0)
        mass = jnp.sum(weights, axis=1, keepdims=True) + jnp.exp(sink_part - peak)
        probs = (weights / mass).astype(BF16)
        mixed[r] = lax.dot_general(
            probs, values, (((1,), (1,)), ((), ())), preferred_element_type=F32
        )
        return carry

    lax.fori_loop(0, rows, attend, 0, unroll=4)
    for h in range(0, q_heads, 2):
        g = h // group
        pair = [mixed[:, h + i, g * hd : (g + 1) * hd] for i in range(2)]
        heads[:, h * hd : (h + 2) * hd] = jnp.concatenate(pair, axis=1).astype(BF16)

    loads[1].wait()
    partial[...] = lax.dot_general(
        heads[...], out_w[...], (((1,), (1,)), ((), ())), preferred_element_type=F32
    )
    part_copies = [send(partial, partial_in.at[q], part_sems, (q,), 0, q) for q in range(1, n_tp)]
    total = partial[...]
    for q in range(1, n_tp):
        part_copies[q - 1].wait()
        total = total + partial_in[q]
    stream = residual[...].astype(F32) + total
    own_stream[...] = stream
    streams[0] = stream.astype(BF16)
    stream_copies = [
        send(streams.at[0], streams.at[k], stream_sems, (k,), k) for k in range(1, n_ep)
    ]

    for copy in meta_copies:
        copy.wait()
    to_smem = pltpu.make_async_copy(meta_all, meta_smem, in_sem)
    to_smem.start()
    to_smem.wait()
    slot_of = [[meta_smem[k, 0, j] for j in range(moves)] for k in range(n_ep)]
    dest_of = [[meta_smem[k, 0, moves + j] for j in range(moves)] for k in range(n_ep)]

    all_rows = n_ep * rows
    new_index = lax.broadcasted_iota(jnp.int32, (all_rows, all_rows), 0)
    old_index = lax.broadcasted_iota(jnp.int32, (all_rows, all_rows), 1)
    home = jnp.where(new_index < rows, new_index, 0)
    for k in range(1, n_ep):
        inside = (new_index >= k * rows) & (new_index < (k + 1) * rows)
        home = jnp.where(inside, new_index + (n_ep - 2 * k) * rows, home)
    source_of = [[None] * moves for _ in range(n_ep)]
    for k in range(n_ep):
        shard = ahead(k)
        receiver = (n_ep - k) % n_ep
        for j in range(moves):
            found = jnp.int32(0)
            leaving = jnp.int32(0)
            for s in range(n_ep):
                hit = dest_of[s][j] == shard
                found = jnp.where(hit, s, found)
                leaving = jnp.where(hit, s * rows + slot_of[s][j], leaving)
            source_of[k][j] = found
            home = jnp.where(new_index == k * rows + slot_of[receiver][j], leaving, home)
    move_to = jnp.where(old_index == home, 1.0, 0.0).astype(BF16)

    for copy in one_copies:
        copy.wait()
    for k in range(n_ep):
        for j in range(moves):
            send2[k, j] = recv1[source_of[k][j], j]
    for copy in stream_copies:
        copy.wait()
    two_copies = [send(send2.at[k], recv2.at[k], two_sems, (k,), k) for k in range(1, n_ep)]
    recv2[0] = send2[0]

    known = streams[...].reshape(all_rows, width)
    wide = known.astype(F32)
    mean_square = jnp.sum(wide * wide, axis=1, keepdims=True) * (1.0 / width)
    tokens = (wide * lax.rsqrt(mean_square + EPSILON) * gain[...]).astype(BF16)
    loads[2].wait()
    gate_part = jnp.dot(tokens, gate_up[:, 0, :], preferred_element_type=F32)
    up_part = jnp.dot(tokens, gate_up[:, 1, :], preferred_element_type=F32)
    hidden[...] = ((up_part + 1.0) * gate_part * jax.nn.sigmoid(ALPHA * gate_part)).astype(BF16)
    moved = jnp.dot(move_to, hidden[...], preferred_element_type=F32).astype(BF16)
    loads[3].wait()
    expert_out = jnp.dot(moved, down_w[...], preferred_element_type=F32)
    for c in range(n_tp):
        ysend[c] = (
            expert_out[:, c * half : (c + 1) * half].astype(BF16).reshape(n_ep, rows, half)
        )
    y_copies = []
    for q in range(n_tp):
        core = lax.rem(tp + q, n_tp)
        for k in range(n_ep):
            if k or q:
                y_copies.append(send(ysend.at[core, k], yrecv.at[q, k], y_sems, (q, k), k, q))
    yrecv[0, 0] = ysend[tp, 0]

    row_index = lax.broadcasted_iota(jnp.int32, (rows, 1), 0)
    kept = row_index >= 0
    for j in range(moves):
        kept = kept & (row_index != slot_of[0][j])
    brought = jnp.dot(move_to[0:rows], known, preferred_element_type=F32)
    new_stream = jnp.where(kept, own_stream[...], brought)
    mean_square = jnp.sum(new_stream * new_stream, axis=1, keepdims=True) * (1.0 / width)
    normed = new_stream * lax.rsqrt(mean_square + EPSILON) * gain[...]
    logits = lax.dot_general(
        normed,
        router[...].astype(F32),
        (((1,), (1,)), ((), ())),
        precision=lax.Precision.HIGHEST,
        preferred_element_type=F32,
    )
    expert_index = lax.broadcasted_iota(jnp.int32, logits.shape, 1)
    chosen = jnp.zeros(logits.shape, F32)
    for t in range(expert_ids.shape[1]):
        chosen = jnp.where(expert_index == expert_ids[:, t : t + 1], 1.0, chosen)
    best = jnp.max(jnp.where(chosen > 0.5, logits, -1e30), axis=1, keepdims=True)
    raised = jnp.where(chosen > 0.5, jnp.exp(logits - best), 0.0)
    gates = raised / jnp.sum(raised, axis=1, keepdims=True)
    result = new_stream[:, 0:half]
    for c in range(1, n_tp):
        result = jnp.where(tp == c, new_stream[:, c * half : (c + 1) * half], result)
    for copy in y_copies:
        copy.wait()
    for k in range(n_ep):
        gate = jnp.sum(
            jnp.where(expert_index == behind(k), gates, 0.0), axis=1, keepdims=True
        )
        summed = yrecv[0, k].astype(F32)
        for q in range(1, n_tp):
            summed = summed + yrecv[q, k].astype(F32)
        result = result + gate * summed
    layer_out[...] = result.astype(BF16)

    for copy in two_copies:
        copy.wait()
    for k in range(n_ep):
        for j in range(moves):
            incoming[j, behind(k)] = recv2[k, j]


def per_device(
    n_ep,
    n_tp,
    residual,
    queries,
    new_kv,
    kv_cache,
    cache_len,
    move_slot,
    move_dest,
    sink_logits,
    out_weight,
    norm_gain,
    router_weight,
    expert_ids,
    gate_up,
    down_weight,
):
    rows, width = residual.shape
    _, _, kv, hd, length = kv_cache.shape
    moves = move_slot.shape[0]
    q_heads = sink_logits.shape[0]
    group = q_heads // kv
    hidden_units = down_weight.shape[1]
    filled = insert_token(kv_cache, new_kv, cache_len)
    pieces = filled.reshape(rows, 2 * kv, hd, length)
    same = jnp.eye(kv, dtype=queries.dtype).reshape(1, kv, 1, kv, 1)
    spread = (queries.reshape(rows, kv, group, 1, hd) * same).reshape(rows, q_heads, kv * hd)
    listing = jnp.concatenate([move_slot, move_dest])
    meta = jnp.broadcast_to(jnp.pad(listing, (0, 128 - 2 * moves)), (8, 128))
    piece = (moves, hd, length)
    half = width // n_tp
    smem = pl.BlockSpec(memory_space=pltpu.SMEM)
    vmem = pl.BlockSpec(memory_space=pltpu.VMEM)
    hbm = pl.BlockSpec(memory_space=pl.ANY)
    dma = pltpu.SemaphoreType.DMA
    layer_out, incoming = pl.pallas_call(
        functools.partial(step_kernel, n_ep, n_tp),
        out_shape=(
            jax.ShapeDtypeStruct((rows, half), BF16),
            jax.ShapeDtypeStruct((moves, 2 * kv, hd, length), BF16),
        ),
        in_specs=[smem] * 2 + [vmem] * 7 + [hbm] * 4,
        out_specs=(vmem, vmem),
        scratch_shapes=[
            pltpu.VMEM(pieces.shape, BF16),
            pltpu.VMEM((width, out_weight.shape[0]), BF16),
            pltpu.VMEM((width, 2, hidden_units), BF16),
            pltpu.VMEM((hidden_units, width), BF16),
            pltpu.VMEM((2 * kv,) + piece, BF16),
            pltpu.VMEM((n_ep,) + piece, BF16),
            pltpu.VMEM((n_ep,) + piece, BF16),
            pltpu.VMEM((n_ep,) + piece, BF16),
            pltpu.VMEM((n_ep, 8, 128), jnp.int32),
            pltpu.SMEM((n_ep, 8, 128), jnp.int32),
            pltpu.VMEM((rows, q_heads, kv * hd), F32),
            pltpu.VMEM((rows, q_heads * hd), BF16),
            pltpu.VMEM((rows, width), F32),
            pltpu.VMEM((n_tp, rows, width), F32),
            pltpu.VMEM((rows, width), F32),
            pltpu.VMEM((n_ep, rows, width), BF16),
            pltpu.VMEM((n_ep * rows, hidden_units), BF16),
            pltpu.VMEM((n_tp, n_ep, rows, half), BF16),
            pltpu.VMEM((n_tp, n_ep, rows, half), BF16),
            dma((4,)),
            dma((2, n_ep)),
            dma((2, n_ep)),
            dma((2, n_ep)),
            dma((2, n_tp)),
            dma((2, n_ep)),
            dma((2, n_tp, n_ep)),
            dma,
        ],
        compiler_params=pltpu.CompilerParams(
            collective_id=0, has_side_effects=True, vmem_limit_bytes=48 * 1024 * 1024
        ),
    )(
        cache_len,
        move_slot,
        meta,
        spread,
        residual,
        sink_logits.reshape(q_heads, 1),
        norm_gain.reshape(1, width),
        router_weight.T,
        expert_ids,
        pieces,
        out_weight.T,
        gate_up[0],
        down_weight[0],
    )
    incoming = incoming.reshape((moves,) + kv_cache.shape[1:])
    cache_out = filled
    for j in range(moves):
        cache_out = lax.dynamic_update_slice(
            cache_out, incoming[j : j + 1], (move_slot[j], 0, 0, 0, 0)
        )
    return layer_out, cache_out


def solution(mesh):
    n_ep, n_tp = mesh.shape["ep"], mesh.shape["tp"]

    def body(*arrays):
        kv_cache, gate_up = arrays[3], arrays[12]
        if 2 * kv_cache.shape[2] == n_ep and gate_up.shape[0] == 1 and n_tp == 2:
            return per_device(n_ep, n_tp, *arrays)
        return per_device_general(*arrays)

    in_specs = (
        P(("groups", "ep"), None),
        P(("groups", "ep"), "tp"),
        P(("groups", "ep"), None, "tp"),
        P(("groups", "ep"), None, "tp", None, None),
        P(("groups", "ep")),
        P(("groups", "ep")),
        P(("groups", "ep")),
        P("tp"),
        P("tp", None),
        P(),
        P(),
        P(("groups", "ep"), None),
        P("ep", None, None, "tp"),
        P("ep", "tp", None),
    )
    out_specs = (P(("groups", "ep"), "tp"), P(("groups", "ep"), None, "tp", None, None))
    return jax.shard_map(
        body, mesh=mesh, in_specs=in_specs, out_specs=out_specs, check_vma=False
    )
```

```python
import functools

import jax
import jax.numpy as jnp
from jax import lax
from jax.experimental import pallas as pl
from jax.experimental.pallas import tpu as pltpu
from jax.sharding import PartitionSpec as P

ALPHA = 1.702
EPSILON = 1e-05


def insert_token(cache_values, new_rows, lengths):
    row_count = cache_values.shape[0]
    kv_count = cache_values.shape[2]
    head_dim = cache_values.shape[3]
    length = cache_values.shape[4]
    fresh_rows = new_rows.reshape(row_count, 2, kv_count, head_dim, 1)
    position_index = lax.broadcasted_iota(jnp.int32, (row_count, 1, 1, 1, length), 4)
    return jnp.where(
        position_index == lengths.reshape(row_count, 1, 1, 1, 1), fresh_rows, cache_values
    )


def attend_rows(queries, cache_values, lengths, sink_logits):
    row_count = cache_values.shape[0]
    kv_count = cache_values.shape[2]
    head_dim = cache_values.shape[3]
    length = cache_values.shape[4]
    group = queries.shape[1] // (kv_count * head_dim)
    query_rows = queries.reshape(row_count, kv_count, group, head_dim)
    scores = jnp.einsum(
        "rgqd,rgdl->rgql", query_rows, cache_values[:, 0], preferred_element_type=jnp.float32
    ) * head_dim ** (-0.5)
    visible = lax.broadcasted_iota(jnp.int32, (row_count, 1, 1, length), 3) <= lengths.reshape(
        row_count, 1, 1, 1
    )
    sink_part = sink_logits.reshape(1, kv_count, group, 1)
    peak_score = jnp.maximum(
        jnp.max(jnp.where(visible, scores, -1e30), axis=3, keepdims=True), sink_part
    )
    weights = jnp.where(visible, jnp.exp(scores - peak_score), 0.0)
    total_mass = jnp.sum(weights, axis=3, keepdims=True) + jnp.exp(sink_part - peak_score)
    probabilities = (weights / total_mass).astype(jnp.bfloat16)
    mixture = jnp.einsum(
        "rgql,rgdl->rgqd", probabilities, cache_values[:, 1], preferred_element_type=jnp.float32
    )
    return mixture.astype(jnp.bfloat16).reshape(row_count, -1)


def migrate(cache_values, residual, queries, lengths, move_slot, move_dest):
    my_shard = lax.axis_index("ep")
    row_count = residual.shape[0]
    move_count = move_slot.shape[0]
    current = (cache_values, residual, queries, lengths)
    leaving = tuple((jnp.take(member, move_slot, axis=0) for member in current))
    piece = (
        lax.all_gather(leaving[0], "ep", axis=0, tiled=True),
        lax.all_gather(leaving[1], "ep", axis=0, tiled=True),
        lax.all_gather(leaving[2], "ep", axis=0, tiled=True),
        lax.all_gather(leaving[3], "ep", axis=0, tiled=True),
        lax.all_gather(move_dest, "ep", axis=0, tiled=True),
    )
    piece_rows = piece[4].shape[0]
    column = jnp.arange(piece_rows, dtype=jnp.int32) % move_count
    target = jnp.where(piece[4] == my_shard, move_slot[column], row_count)
    return tuple(
        (held.at[target].set(incoming, mode="drop") for held, incoming in zip(current, piece[:4]))
    )


def per_device_general(
    residual,
    queries,
    new_kv,
    kv_cache,
    cache_len,
    move_slot,
    move_dest,
    sink_logits,
    out_weight,
    norm_gain,
    router_weight,
    expert_ids,
    gate_up,
    down_weight,
):
    row_count = residual.shape[0]
    filled = insert_token(kv_cache, new_kv, cache_len)
    cache_new, resid_new, query_new, length_new = migrate(
        filled, residual, queries, cache_len, move_slot, move_dest
    )
    heads = attend_rows(query_new, cache_new, length_new, sink_logits)
    partial_out = jnp.dot(heads, out_weight, preferred_element_type=jnp.float32)
    stream = resid_new.astype(jnp.float32) + lax.psum(partial_out, "tp")
    mean_square = jnp.mean(stream * stream, axis=1, keepdims=True)
    normed = stream * lax.rsqrt(mean_square + EPSILON) * norm_gain
    tokens = normed.astype(jnp.bfloat16)
    logits = jnp.dot(normed, router_weight.astype(jnp.float32), precision=lax.Precision.HIGHEST)
    raised = jnp.exp(jnp.take_along_axis(logits, expert_ids, axis=1))
    gate_weights = raised / jnp.sum(raised, axis=1, keepdims=True)
    top_count = expert_ids.shape[1]
    expert_count = router_weight.shape[1]
    width = tokens.shape[1]
    capacity = max(2, min(row_count, 2 * row_count * top_count // expert_count))
    flat_ids = expert_ids.reshape(-1)
    onehot = (flat_ids[:, None] == jnp.arange(expert_count, dtype=jnp.int32)[None, :]).astype(
        jnp.int32
    )
    slot_rank = jnp.sum((jnp.cumsum(onehot, axis=0) - 1) * onehot, axis=1)
    position = flat_ids * capacity + slot_rank
    owner_row = jnp.arange(row_count * top_count, dtype=jnp.int32) // top_count
    outgoing = (
        jnp.zeros((expert_count * capacity, width), jnp.bfloat16)
        .at[position]
        .set(tokens[owner_row])
    )
    outgoing = outgoing.reshape(expert_count, capacity, width)
    local_experts = gate_up.shape[0]
    share_width = width // lax.axis_size("tp")
    offset = lax.axis_index("tp") * share_width
    features = lax.all_to_all(outgoing, "ep", split_axis=0, concat_axis=0, tiled=True)
    slot_count = features.shape[1]
    grouped = features.reshape(-1, local_experts, slot_count, features.shape[2])
    gate_and_up = jnp.einsum(
        "secd,edkf->seckf", grouped, gate_up, preferred_element_type=jnp.float32
    )
    gate_part = gate_and_up[:, :, :, 0, :]
    up_part = gate_and_up[:, :, :, 1, :]
    hidden = ((up_part + 1.0) * gate_part * jax.nn.sigmoid(ALPHA * gate_part)).astype(jnp.bfloat16)
    partial_down = jnp.einsum(
        "secf,efd->secd", hidden, down_weight, preferred_element_type=jnp.float32
    )
    summed = lax.psum_scatter(
        partial_down.reshape(-1, slot_count, partial_down.shape[3]),
        "tp",
        scatter_dimension=2,
        tiled=True,
    )
    returned = lax.all_to_all(
        summed.astype(jnp.bfloat16), "ep", split_axis=0, concat_axis=0, tiled=True
    )
    back_rows = returned.reshape(expert_count * capacity, -1)[position].astype(jnp.float32)
    mixture = jnp.sum(
        back_rows.reshape(row_count, top_count, -1) * gate_weights[:, :, None], axis=1
    )
    own_stream = lax.dynamic_slice_in_dim(stream, offset, share_width, 1)
    layer_out = (own_stream + mixture).astype(jnp.bfloat16)
    return (layer_out, cache_new)


MESH = pl.DeviceIdType.MESH
F32 = jnp.float32
BF16 = jnp.bfloat16


def wrap(value, size):
    value = jnp.where(value < 0, value + size, value)
    return jnp.where(value >= size, value - size, value)


def step_kernel(
    n_ep,
    n_tp,
    lengths,
    slots,
    dests,
    sink,
    queries,
    new_kv,
    residual,
    gain,
    router,
    expert_ids,
    cache_hbm,
    out_hbm,
    gate_up_hbm,
    down_hbm,
    layer_out,
    incoming,
    filled,
    meta,
    spread,
    cache,
    out_w,
    gate_up,
    gate_w,
    up_w,
    down_w,
    send1,
    recv1,
    send2,
    recv2,
    meta_all,
    meta_smem,
    mixed,
    heads,
    partial,
    partial_in,
    own_stream,
    streams,
    hidden,
    ysend,
    yrecv,
    local_sem,
    meta_sems,
    one_sems,
    two_sems,
    part_sems,
    stream_sems,
    y_sems,
    in_sem,
    out_sem,
):
    ep = lax.axis_index("ep")
    tp = lax.axis_index("tp")
    rows, q_heads, lanes = mixed.shape
    width = residual.shape[1]
    half = width // n_tp
    pieces = cache.shape[1]
    kv = pieces // 2
    hd = cache.shape[2]
    moves = send1.shape[1]
    group = q_heads // kv

    def ahead(k):
        return lax.rem(ep + k, n_ep)

    def behind(k):
        return lax.rem(ep - k + n_ep, n_ep)

    loads = [
        pltpu.make_async_copy(cache_hbm, cache, local_sem.at[0]),
        pltpu.make_async_copy(out_hbm, out_w, local_sem.at[1]),
        pltpu.make_async_copy(gate_up_hbm, gate_up, local_sem.at[2]),
        pltpu.make_async_copy(down_hbm, down_w, local_sem.at[3]),
    ]
    for load in loads:
        load.start()

    lane = lax.broadcasted_iota(jnp.int32, meta.shape, 1)
    listing = jnp.zeros(meta.shape, jnp.int32)
    for j in range(moves):
        listing = jnp.where(lane == j, slots[j], listing)
        listing = jnp.where(lane == moves + j, dests[j], listing)
    meta[...] = listing

    barrier = pltpu.get_barrier_semaphore()
    for k in range(n_ep):
        for q in range(n_tp):
            if k or q:
                pl.semaphore_signal(
                    barrier,
                    inc=1,
                    device_id={"ep": ahead(k), "tp": lax.rem(tp + q, n_tp)},
                    device_id_type=MESH,
                )

    def send(src, dst, sems, index, k, q=0):
        target = {"ep": ahead(k)} if k else {}
        if q:
            target["tp"] = lax.rem(tp + q, n_tp)
        copy = pltpu.make_async_remote_copy(
            src_ref=src,
            dst_ref=dst,
            send_sem=sems.at[(0,) + index],
            recv_sem=sems.at[(1,) + index],
            device_id=target,
            device_id_type=MESH,
        )
        copy.start()
        return copy

    fresh = [new_kv[:, i, :] for i in range(2)]
    length = cache.shape[3]
    row_of = lax.broadcasted_iota(jnp.int32, (rows, length), 0)
    place_of = lax.broadcasted_iota(jnp.int32, (rows, length), 1)
    place = lax.broadcasted_iota(jnp.int32, (kv * hd, length), 1)

    def inserted(raw, i, r, last):
        spot = jnp.where((row_of == r) & (place_of == last), 1.0, 0.0).astype(BF16)
        column = lax.dot_general(
            fresh[i], spot, (((0,), (0,)), ((), ())), preferred_element_type=F32
        )
        raw = raw.reshape(kv * hd, length).astype(F32)
        return jnp.where(place == last, column, raw).astype(BF16)

    loads[0].wait()
    for j in range(moves):
        slot = slots[j]
        for i in range(2):
            part = inserted(cache[slot, i * kv : (i + 1) * kv], i, slot, lengths[slot])
            part = part.reshape(kv, hd, length)
            for g in range(kv):
                send1[i * kv + g, j] = part[g]
    pl.semaphore_wait(barrier, n_ep * n_tp - 1)
    meta_copies = [send(meta, meta_all.at[k], meta_sems, (k,), k) for k in range(1, n_ep)]
    meta_all[0] = meta[...]
    one_copies = [
        send(send1.at[ahead(k)], recv1.at[k], one_sems, (k,), k) for k in range(1, n_ep)
    ]
    recv1[0] = send1[ep]

    position_index = lax.broadcasted_iota(jnp.int32, (q_heads, length), 1)
    head_index = lax.broadcasted_iota(jnp.int32, (q_heads, 1), 0)
    sink_part = jnp.zeros((q_heads, 1), F32)
    for h in range(q_heads):
        sink_part = jnp.where(head_index == h, sink[h], sink_part)
    spread[...] = jnp.zeros(spread.shape, F32)
    wide_queries = queries[...].astype(F32)
    for h in range(q_heads):
        g = h // group
        spread[:, h, g * hd : (g + 1) * hd] = wide_queries[:, h * hd : (h + 1) * hd]

    def attend(r, carry):
        last = lengths[r]
        keys = inserted(cache[r, 0:kv], 0, r, last)
        values = inserted(cache[r, kv : 2 * kv], 1, r, last)
        cache[r, 0:kv] = keys.reshape(kv, hd, length)
        cache[r, kv : 2 * kv] = values.reshape(kv, hd, length)
        asked = spread[r].astype(BF16)
        scores = jnp.dot(asked, keys, preferred_element_type=F32) * hd ** (-0.5)
        visible = position_index <= last
        peak = jnp.maximum(
            jnp.max(jnp.where(visible, scores, -1e30), axis=1, keepdims=True), sink_part
        )
        weights = jnp.where(visible, jnp.exp(scores - peak), 0.0)
        mass = jnp.sum(weights, axis=1, keepdims=True) + jnp.exp(sink_part - peak)
        probs = (weights / mass).astype(BF16)
        mixed[r] = lax.dot_general(
            probs, values, (((1,), (1,)), ((), ())), preferred_element_type=F32
        )
        return carry

    lax.fori_loop(0, rows, attend, 0, unroll=4)
    store = pltpu.make_async_copy(cache, filled, out_sem)
    store.start()
    for h in range(0, q_heads, 2):
        g = h // group
        pair = [mixed[:, h + i, g * hd : (g + 1) * hd] for i in range(2)]
        heads[:, h * hd : (h + 2) * hd] = jnp.concatenate(pair, axis=1).astype(BF16)

    loads[1].wait()
    partial[...] = lax.dot_general(
        heads[...], out_w[...], (((1,), (1,)), ((), ())), preferred_element_type=F32
    )
    part_copies = [send(partial, partial_in.at[q], part_sems, (q,), 0, q) for q in range(1, n_tp)]
    loads[2].wait()
    gate_w[...] = gate_up[:, 0, :]
    total = partial[...]
    for q in range(1, n_tp):
        part_copies[q - 1].wait()
        total = total + partial_in[q]
    stream = residual[...].astype(F32) + total
    own_stream[...] = stream
    streams[0] = stream.astype(BF16)
    stream_copies = [
        send(streams.at[0], streams.at[k], stream_sems, (k,), k) for k in range(1, n_ep)
    ]

    up_w[...] = gate_up[:, 1, :]

    for copy in meta_copies:
        copy.wait()
    to_smem = pltpu.make_async_copy(meta_all, meta_smem, in_sem)
    to_smem.start()
    to_smem.wait()
    slot_of = [[meta_smem[k, 0, j] for j in range(moves)] for k in range(n_ep)]
    dest_of = [[meta_smem[k, 0, moves + j] for j in range(moves)] for k in range(n_ep)]

    all_rows = n_ep * rows
    new_index = lax.broadcasted_iota(jnp.int32, (all_rows, all_rows), 0)
    old_index = lax.broadcasted_iota(jnp.int32, (all_rows, all_rows), 1)
    home = jnp.where(new_index < rows, new_index, 0)
    for k in range(1, n_ep):
        inside = (new_index >= k * rows) & (new_index < (k + 1) * rows)
        home = jnp.where(inside, new_index + (n_ep - 2 * k) * rows, home)
    source_of = [[None] * moves for _ in range(n_ep)]
    for k in range(n_ep):
        shard = ahead(k)
        receiver = (n_ep - k) % n_ep
        for j in range(moves):
            found = jnp.int32(0)
            leaving = jnp.int32(0)
            for s in range(n_ep):
                hit = dest_of[s][j] == shard
                found = jnp.where(hit, s, found)
                leaving = jnp.where(hit, s * rows + slot_of[s][j], leaving)
            source_of[k][j] = found
            home = jnp.where(new_index == k * rows + slot_of[receiver][j], leaving, home)
    move_to = jnp.where(old_index == home, 1.0, 0.0).astype(BF16)

    for copy in one_copies:
        copy.wait()
    for k in range(n_ep):
        for j in range(moves):
            send2[k, j] = recv1[source_of[k][j], j]
    for copy in stream_copies:
        copy.wait()
    two_copies = [send(send2.at[k], recv2.at[k], two_sems, (k,), k) for k in range(1, n_ep)]
    recv2[0] = send2[0]

    gain_row = gain[...].reshape(1, width)
    known = streams[...].reshape(all_rows, width)
    wide = known.astype(F32)
    mean_square = jnp.sum(wide * wide, axis=1, keepdims=True) * (1.0 / width)
    tokens = (wide * lax.rsqrt(mean_square + EPSILON) * gain_row).astype(BF16)
    gate_part = jnp.dot(tokens, gate_w[...], preferred_element_type=F32)
    up_part = jnp.dot(tokens, up_w[...], preferred_element_type=F32)
    hidden[...] = ((up_part + 1.0) * gate_part * jax.nn.sigmoid(ALPHA * gate_part)).astype(BF16)
    moved = jnp.dot(move_to, hidden[...], preferred_element_type=F32).astype(BF16)
    loads[3].wait()
    expert_out = jnp.dot(moved, down_w[...], preferred_element_type=F32)
    for c in range(n_tp):
        ysend[c] = (
            expert_out[:, c * half : (c + 1) * half].astype(BF16).reshape(n_ep, rows, half)
        )
    y_copies = []
    for q in range(n_tp):
        core = lax.rem(tp + q, n_tp)
        for k in range(n_ep):
            if k or q:
                y_copies.append(send(ysend.at[core, k], yrecv.at[q, k], y_sems, (q, k), k, q))
    yrecv[0, 0] = ysend[tp, 0]

    row_index = lax.broadcasted_iota(jnp.int32, (rows, 1), 0)
    kept = row_index >= 0
    for j in range(moves):
        kept = kept & (row_index != slot_of[0][j])
    brought = jnp.dot(move_to[0:rows], known, preferred_element_type=F32)
    new_stream = jnp.where(kept, own_stream[...], brought)
    mean_square = jnp.sum(new_stream * new_stream, axis=1, keepdims=True) * (1.0 / width)
    normed = new_stream * lax.rsqrt(mean_square + EPSILON) * gain_row
    logits = lax.dot_general(
        router[...].astype(F32),
        normed,
        (((1,), (1,)), ((), ())),
        precision=lax.Precision.HIGHEST,
        preferred_element_type=F32,
    )
    expert_index = lax.broadcasted_iota(jnp.int32, logits.shape, 0)
    chosen = jnp.zeros(logits.shape, F32)
    for t in range(expert_ids.shape[0]):
        chosen = jnp.where(expert_index == expert_ids[t : t + 1, :], 1.0, chosen)
    best = jnp.max(jnp.where(chosen > 0.5, logits, -1e30), axis=0, keepdims=True)
    raised = jnp.where(chosen > 0.5, jnp.exp(logits - best), 0.0)
    gates = raised / jnp.sum(raised, axis=0, keepdims=True)
    slot_index = lax.broadcasted_iota(jnp.int32, (n_ep, n_ep), 1)
    owner = lax.broadcasted_iota(jnp.int32, (n_ep, n_ep), 0)
    order = jnp.where(wrap(ep - slot_index, n_ep) == owner, 1.0, 0.0)
    by_slot = lax.dot_general(
        gates,
        order,
        (((0,), (0,)), ((), ())),
        precision=lax.Precision.HIGHEST,
        preferred_element_type=F32,
    )
    result = new_stream[:, 0:half]
    for c in range(1, n_tp):
        result = jnp.where(tp == c, new_stream[:, c * half : (c + 1) * half], result)
    for copy in y_copies:
        copy.wait()
    for k in range(n_ep):
        gate = by_slot[:, k : k + 1]
        summed = yrecv[0, k].astype(F32)
        for q in range(1, n_tp):
            summed = summed + yrecv[q, k].astype(F32)
        result = result + gate * summed
    layer_out[...] = result.astype(BF16)

    for copy in two_copies:
        copy.wait()
    for k in range(n_ep):
        for j in range(moves):
            incoming[j, behind(k)] = recv2[k, j]
    store.wait()


def per_device(
    n_ep,
    n_tp,
    residual,
    queries,
    new_kv,
    kv_cache,
    cache_len,
    move_slot,
    move_dest,
    sink_logits,
    out_weight,
    norm_gain,
    router_weight,
    expert_ids,
    gate_up,
    down_weight,
):
    rows, width = residual.shape
    _, _, kv, hd, length = kv_cache.shape
    moves = move_slot.shape[0]
    q_heads = sink_logits.shape[0]
    hidden_units = down_weight.shape[1]
    pieces = kv_cache.reshape(rows, 2 * kv, hd, length)
    piece = (moves, hd, length)
    half = width // n_tp
    smem = pl.BlockSpec(memory_space=pltpu.SMEM)
    vmem = pl.BlockSpec(memory_space=pltpu.VMEM)
    hbm = pl.BlockSpec(memory_space=pl.ANY)
    dma = pltpu.SemaphoreType.DMA
    layer_out, incoming, filled = pl.pallas_call(
        functools.partial(step_kernel, n_ep, n_tp),
        out_shape=(
            jax.ShapeDtypeStruct((rows, half), BF16),
            jax.ShapeDtypeStruct((moves, 2 * kv, hd, length), BF16),
            jax.ShapeDtypeStruct(pieces.shape, BF16),
        ),
        in_specs=[smem] * 4 + [vmem] * 6 + [hbm] * 4,
        out_specs=(vmem, vmem, hbm),
        scratch_shapes=[
            pltpu.VMEM((8, 128), jnp.int32),
            pltpu.VMEM((rows, q_heads, kv * hd), F32),
            pltpu.VMEM(pieces.shape, BF16),
            pltpu.VMEM((width, out_weight.shape[0]), BF16),
            pltpu.VMEM((width, 2, hidden_units), BF16),
            pltpu.VMEM((width, hidden_units), BF16),
            pltpu.VMEM((width, hidden_units), BF16),
            pltpu.VMEM((hidden_units, width), BF16),
            pltpu.VMEM((2 * kv,) + piece, BF16),
            pltpu.VMEM((n_ep,) + piece, BF16),
            pltpu.VMEM((n_ep,) + piece, BF16),
            pltpu.VMEM((n_ep,) + piece, BF16),
            pltpu.VMEM((n_ep, 8, 128), jnp.int32),
            pltpu.SMEM((n_ep, 8, 128), jnp.int32),
            pltpu.VMEM((rows, q_heads, kv * hd), F32),
            pltpu.VMEM((rows, q_heads * hd), BF16),
            pltpu.VMEM((rows, width), F32),
            pltpu.VMEM((n_tp, rows, width), F32),
            pltpu.VMEM((rows, width), F32),
            pltpu.VMEM((n_ep, rows, width), BF16),
            pltpu.VMEM((n_ep * rows, hidden_units), BF16),
            pltpu.VMEM((n_tp, n_ep, rows, half), BF16),
            pltpu.VMEM((n_tp, n_ep, rows, half), BF16),
            dma((4,)),
            dma((2, n_ep)),
            dma((2, n_ep)),
            dma((2, n_ep)),
            dma((2, n_tp)),
            dma((2, n_ep)),
            dma((2, n_tp, n_ep)),
            dma,
            dma,
        ],
        compiler_params=pltpu.CompilerParams(
            collective_id=0, has_side_effects=True, vmem_limit_bytes=58 * 1024 * 1024
        ),
    )(
        cache_len,
        move_slot,
        move_dest,
        sink_logits,
        queries,
        new_kv,
        residual,
        norm_gain,
        router_weight.T,
        expert_ids.T,
        pieces,
        out_weight.T,
        gate_up[0],
        down_weight[0],
    )
    row_index = lax.broadcasted_iota(jnp.int32, (rows, 1, 1, 1), 0)
    cache_out = filled
    for j in range(moves):
        cache_out = jnp.where(row_index == move_slot[j], incoming[j][None], cache_out)
    cache_out = cache_out.reshape(kv_cache.shape)
    return layer_out, cache_out


def solution(mesh):
    n_ep, n_tp = mesh.shape["ep"], mesh.shape["tp"]

    def body(*arrays):
        kv_cache, gate_up = arrays[3], arrays[12]
        if 2 * kv_cache.shape[2] == n_ep and gate_up.shape[0] == 1 and n_tp == 2:
            return per_device(n_ep, n_tp, *arrays)
        return per_device_general(*arrays)

    in_specs = (
        P(("groups", "ep"), None),
        P(("groups", "ep"), "tp"),
        P(("groups", "ep"), None, "tp"),
        P(("groups", "ep"), None, "tp", None, None),
        P(("groups", "ep")),
        P(("groups", "ep")),
        P(("groups", "ep")),
        P("tp"),
        P("tp", None),
        P(),
        P(),
        P(("groups", "ep"), None),
        P("ep", None, None, "tp"),
        P("ep", "tp", None),
    )
    out_specs = (P(("groups", "ep"), "tp"), P(("groups", "ep"), None, "tp", None, None))
    return jax.shard_map(
        body, mesh=mesh, in_specs=in_specs, out_specs=out_specs, check_vma=False
    )
```

```python
import functools

import jax
import jax.numpy as jnp
from jax import lax
from jax.experimental import pallas as pl
from jax.experimental.pallas import tpu as pltpu
from jax.sharding import PartitionSpec as P

ALPHA = 1.702
EPSILON = 1e-05


def insert_token(cache_values, new_rows, lengths):
    row_count = cache_values.shape[0]
    kv_count = cache_values.shape[2]
    head_dim = cache_values.shape[3]
    length = cache_values.shape[4]
    fresh_rows = new_rows.reshape(row_count, 2, kv_count, head_dim, 1)
    position_index = lax.broadcasted_iota(jnp.int32, (row_count, 1, 1, 1, length), 4)
    return jnp.where(
        position_index == lengths.reshape(row_count, 1, 1, 1, 1), fresh_rows, cache_values
    )


def attend_rows(queries, cache_values, lengths, sink_logits):
    row_count = cache_values.shape[0]
    kv_count = cache_values.shape[2]
    head_dim = cache_values.shape[3]
    length = cache_values.shape[4]
    group = queries.shape[1] // (kv_count * head_dim)
    query_rows = queries.reshape(row_count, kv_count, group, head_dim)
    scores = jnp.einsum(
        "rgqd,rgdl->rgql", query_rows, cache_values[:, 0], preferred_element_type=jnp.float32
    ) * head_dim ** (-0.5)
    visible = lax.broadcasted_iota(jnp.int32, (row_count, 1, 1, length), 3) <= lengths.reshape(
        row_count, 1, 1, 1
    )
    sink_part = sink_logits.reshape(1, kv_count, group, 1)
    peak_score = jnp.maximum(
        jnp.max(jnp.where(visible, scores, -1e30), axis=3, keepdims=True), sink_part
    )
    weights = jnp.where(visible, jnp.exp(scores - peak_score), 0.0)
    total_mass = jnp.sum(weights, axis=3, keepdims=True) + jnp.exp(sink_part - peak_score)
    probabilities = (weights / total_mass).astype(jnp.bfloat16)
    mixture = jnp.einsum(
        "rgql,rgdl->rgqd", probabilities, cache_values[:, 1], preferred_element_type=jnp.float32
    )
    return mixture.astype(jnp.bfloat16).reshape(row_count, -1)


def migrate(cache_values, residual, queries, lengths, move_slot, move_dest):
    my_shard = lax.axis_index("ep")
    row_count = residual.shape[0]
    move_count = move_slot.shape[0]
    current = (cache_values, residual, queries, lengths)
    leaving = tuple((jnp.take(member, move_slot, axis=0) for member in current))
    piece = (
        lax.all_gather(leaving[0], "ep", axis=0, tiled=True),
        lax.all_gather(leaving[1], "ep", axis=0, tiled=True),
        lax.all_gather(leaving[2], "ep", axis=0, tiled=True),
        lax.all_gather(leaving[3], "ep", axis=0, tiled=True),
        lax.all_gather(move_dest, "ep", axis=0, tiled=True),
    )
    piece_rows = piece[4].shape[0]
    column = jnp.arange(piece_rows, dtype=jnp.int32) % move_count
    target = jnp.where(piece[4] == my_shard, move_slot[column], row_count)
    return tuple(
        (held.at[target].set(incoming, mode="drop") for held, incoming in zip(current, piece[:4]))
    )


def per_device_general(
    residual,
    queries,
    new_kv,
    kv_cache,
    cache_len,
    move_slot,
    move_dest,
    sink_logits,
    out_weight,
    norm_gain,
    router_weight,
    expert_ids,
    gate_up,
    down_weight,
):
    row_count = residual.shape[0]
    filled = insert_token(kv_cache, new_kv, cache_len)
    cache_new, resid_new, query_new, length_new = migrate(
        filled, residual, queries, cache_len, move_slot, move_dest
    )
    heads = attend_rows(query_new, cache_new, length_new, sink_logits)
    partial_out = jnp.dot(heads, out_weight, preferred_element_type=jnp.float32)
    stream = resid_new.astype(jnp.float32) + lax.psum(partial_out, "tp")
    mean_square = jnp.mean(stream * stream, axis=1, keepdims=True)
    normed = stream * lax.rsqrt(mean_square + EPSILON) * norm_gain
    tokens = normed.astype(jnp.bfloat16)
    logits = jnp.dot(normed, router_weight.astype(jnp.float32), precision=lax.Precision.HIGHEST)
    raised = jnp.exp(jnp.take_along_axis(logits, expert_ids, axis=1))
    gate_weights = raised / jnp.sum(raised, axis=1, keepdims=True)
    top_count = expert_ids.shape[1]
    expert_count = router_weight.shape[1]
    width = tokens.shape[1]
    capacity = max(2, min(row_count, 2 * row_count * top_count // expert_count))
    flat_ids = expert_ids.reshape(-1)
    onehot = (flat_ids[:, None] == jnp.arange(expert_count, dtype=jnp.int32)[None, :]).astype(
        jnp.int32
    )
    slot_rank = jnp.sum((jnp.cumsum(onehot, axis=0) - 1) * onehot, axis=1)
    position = flat_ids * capacity + slot_rank
    owner_row = jnp.arange(row_count * top_count, dtype=jnp.int32) // top_count
    outgoing = (
        jnp.zeros((expert_count * capacity, width), jnp.bfloat16)
        .at[position]
        .set(tokens[owner_row])
    )
    outgoing = outgoing.reshape(expert_count, capacity, width)
    local_experts = gate_up.shape[0]
    share_width = width // lax.axis_size("tp")
    offset = lax.axis_index("tp") * share_width
    features = lax.all_to_all(outgoing, "ep", split_axis=0, concat_axis=0, tiled=True)
    slot_count = features.shape[1]
    grouped = features.reshape(-1, local_experts, slot_count, features.shape[2])
    gate_and_up = jnp.einsum(
        "secd,edkf->seckf", grouped, gate_up, preferred_element_type=jnp.float32
    )
    gate_part = gate_and_up[:, :, :, 0, :]
    up_part = gate_and_up[:, :, :, 1, :]
    hidden = ((up_part + 1.0) * gate_part * jax.nn.sigmoid(ALPHA * gate_part)).astype(jnp.bfloat16)
    partial_down = jnp.einsum(
        "secf,efd->secd", hidden, down_weight, preferred_element_type=jnp.float32
    )
    summed = lax.psum_scatter(
        partial_down.reshape(-1, slot_count, partial_down.shape[3]),
        "tp",
        scatter_dimension=2,
        tiled=True,
    )
    returned = lax.all_to_all(
        summed.astype(jnp.bfloat16), "ep", split_axis=0, concat_axis=0, tiled=True
    )
    back_rows = returned.reshape(expert_count * capacity, -1)[position].astype(jnp.float32)
    mixture = jnp.sum(
        back_rows.reshape(row_count, top_count, -1) * gate_weights[:, :, None], axis=1
    )
    own_stream = lax.dynamic_slice_in_dim(stream, offset, share_width, 1)
    layer_out = (own_stream + mixture).astype(jnp.bfloat16)
    return (layer_out, cache_new)


MESH = pl.DeviceIdType.MESH
F32 = jnp.float32
BF16 = jnp.bfloat16


def wrap(value, size):
    value = jnp.where(value < 0, value + size, value)
    return jnp.where(value >= size, value - size, value)


def step_kernel(
    n_ep,
    n_tp,
    lengths,
    slots,
    dests,
    sink,
    queries,
    new_kv,
    residual,
    gain,
    router,
    expert_ids,
    cache_hbm,
    out_hbm,
    gate_up_hbm,
    down_hbm,
    layer_out,
    incoming,
    filled,
    meta,
    spread,
    cache,
    out_w,
    gate_up,
    gate_w,
    up_w,
    down_w,
    send1,
    recv1,
    send2,
    recv2,
    meta_all,
    meta_smem,
    mixed,
    heads,
    partial,
    partial_in,
    own_stream,
    streams,
    hidden,
    ysend,
    yrecv,
    local_sem,
    meta_sems,
    one_sems,
    two_sems,
    part_sems,
    stream_sems,
    y_sems,
    in_sem,
    out_sem,
):
    ep = lax.axis_index("ep")
    tp = lax.axis_index("tp")
    rows, q_heads, lanes = mixed.shape
    width = residual.shape[1]
    half = width // n_tp
    pieces = cache.shape[1]
    kv = pieces // 2
    hd = cache.shape[2]
    moves = send1.shape[1]
    group = q_heads // kv

    def ahead(k):
        return lax.rem(ep + k, n_ep)

    def behind(k):
        return lax.rem(ep - k + n_ep, n_ep)

    loads = [
        pltpu.make_async_copy(cache_hbm, cache, local_sem.at[0]),
        pltpu.make_async_copy(out_hbm, out_w, local_sem.at[1]),
        pltpu.make_async_copy(gate_up_hbm, gate_up, local_sem.at[2]),
        pltpu.make_async_copy(down_hbm, down_w, local_sem.at[3]),
    ]
    for load in loads:
        load.start()

    lane = lax.broadcasted_iota(jnp.int32, meta.shape, 1)
    listing = jnp.zeros(meta.shape, jnp.int32)
    for j in range(moves):
        listing = jnp.where(lane == j, slots[j], listing)
        listing = jnp.where(lane == moves + j, dests[j], listing)
    meta[...] = listing

    barrier = pltpu.get_barrier_semaphore()
    for k in range(n_ep):
        for q in range(n_tp):
            if k or q:
                pl.semaphore_signal(
                    barrier,
                    inc=1,
                    device_id={"ep": ahead(k), "tp": lax.rem(tp + q, n_tp)},
                    device_id_type=MESH,
                )

    def send(src, dst, sems, index, k, q=0):
        target = {"ep": ahead(k)} if k else {}
        if q:
            target["tp"] = lax.rem(tp + q, n_tp)
        copy = pltpu.make_async_remote_copy(
            src_ref=src,
            dst_ref=dst,
            send_sem=sems.at[(0,) + index],
            recv_sem=sems.at[(1,) + index],
            device_id=target,
            device_id_type=MESH,
        )
        copy.start()
        return copy

    fresh = [new_kv[:, i, :] for i in range(2)]
    length = cache.shape[3]
    row_of = lax.broadcasted_iota(jnp.int32, (rows, length), 0)
    place_of = lax.broadcasted_iota(jnp.int32, (rows, length), 1)
    place = lax.broadcasted_iota(jnp.int32, (kv * hd, length), 1)

    def inserted(raw, i, r, last):
        spot = jnp.where((row_of == r) & (place_of == last), 1.0, 0.0).astype(BF16)
        column = lax.dot_general(
            fresh[i], spot, (((0,), (0,)), ((), ())), preferred_element_type=F32
        )
        raw = raw.reshape(kv * hd, length).astype(F32)
        return jnp.where(place == last, column, raw).astype(BF16)

    loads[0].wait()
    for j in range(moves):
        slot = slots[j]
        for i in range(2):
            part = inserted(cache[slot, i * kv : (i + 1) * kv], i, slot, lengths[slot])
            part = part.reshape(kv, hd, length)
            for g in range(kv):
                send1[i * kv + g, j] = part[g]
    pl.semaphore_wait(barrier, n_ep * n_tp - 1)
    meta_copies = [send(meta, meta_all.at[k], meta_sems, (k,), k) for k in range(1, n_ep)]
    meta_all[0] = meta[...]
    one_copies = [
        send(send1.at[ahead(k)], recv1.at[k], one_sems, (k,), k) for k in range(1, n_ep)
    ]
    recv1[0] = send1[ep]

    position_index = lax.broadcasted_iota(jnp.int32, (q_heads, length), 1)
    head_index = lax.broadcasted_iota(jnp.int32, (q_heads, 1), 0)
    sink_part = jnp.zeros((q_heads, 1), F32)
    for h in range(q_heads):
        sink_part = jnp.where(head_index == h, sink[h], sink_part)
    spread[...] = jnp.zeros(spread.shape, F32)
    wide_queries = queries[...].astype(F32)
    for h in range(q_heads):
        g = h // group
        spread[:, h, g * hd : (g + 1) * hd] = wide_queries[:, h * hd : (h + 1) * hd]

    def attend(r, carry):
        last = lengths[r]
        keys = inserted(cache[r, 0:kv], 0, r, last)
        values = inserted(cache[r, kv : 2 * kv], 1, r, last)
        cache[r, 0:kv] = keys.reshape(kv, hd, length)
        cache[r, kv : 2 * kv] = values.reshape(kv, hd, length)
        asked = spread[r].astype(BF16)
        scores = jnp.dot(asked, keys, preferred_element_type=F32) * hd ** (-0.5)
        visible = position_index <= last
        peak = jnp.maximum(
            jnp.max(jnp.where(visible, scores, -1e30), axis=1, keepdims=True), sink_part
        )
        weights = jnp.where(visible, jnp.exp(scores - peak), 0.0)
        mass = jnp.sum(weights, axis=1, keepdims=True) + jnp.exp(sink_part - peak)
        probs = (weights / mass).astype(BF16)
        mixed[r] = lax.dot_general(
            probs, values, (((1,), (1,)), ((), ())), preferred_element_type=F32
        )
        return carry

    lax.fori_loop(0, rows, attend, 0, unroll=4)
    store = pltpu.make_async_copy(cache, filled, out_sem)
    store.start()
    for h in range(0, q_heads, 2):
        g = h // group
        pair = [mixed[:, h + i, g * hd : (g + 1) * hd] for i in range(2)]
        heads[:, h * hd : (h + 2) * hd] = jnp.concatenate(pair, axis=1).astype(BF16)

    loads[1].wait()
    partial[...] = lax.dot_general(
        heads[...], out_w[...], (((1,), (1,)), ((), ())), preferred_element_type=F32
    )
    part_copies = [send(partial, partial_in.at[q], part_sems, (q,), 0, q) for q in range(1, n_tp)]
    loads[2].wait()
    gate_w[...] = gate_up[:, 0, :]
    total = partial[...]
    for q in range(1, n_tp):
        part_copies[q - 1].wait()
        total = total + partial_in[q]
    stream = residual[...].astype(F32) + total
    own_stream[...] = stream
    streams[0] = stream.astype(BF16)
    stream_copies = [
        send(streams.at[0], streams.at[k], stream_sems, (k,), k) for k in range(1, n_ep)
    ]

    up_w[...] = gate_up[:, 1, :]

    for copy in meta_copies:
        copy.wait()
    to_smem = pltpu.make_async_copy(meta_all, meta_smem, in_sem)
    to_smem.start()
    to_smem.wait()
    slot_of = [[meta_smem[k, 0, j] for j in range(moves)] for k in range(n_ep)]
    dest_of = [[meta_smem[k, 0, moves + j] for j in range(moves)] for k in range(n_ep)]

    all_rows = n_ep * rows
    new_index = lax.broadcasted_iota(jnp.int32, (all_rows, all_rows), 0)
    old_index = lax.broadcasted_iota(jnp.int32, (all_rows, all_rows), 1)
    home = jnp.where(new_index < rows, new_index, 0)
    for k in range(1, n_ep):
        inside = (new_index >= k * rows) & (new_index < (k + 1) * rows)
        home = jnp.where(inside, new_index + (n_ep - 2 * k) * rows, home)
    source_of = [[None] * moves for _ in range(n_ep)]
    for k in range(n_ep):
        shard = ahead(k)
        receiver = (n_ep - k) % n_ep
        for j in range(moves):
            found = jnp.int32(0)
            leaving = jnp.int32(0)
            for s in range(n_ep):
                hit = dest_of[s][j] == shard
                found = jnp.where(hit, s, found)
                leaving = jnp.where(hit, s * rows + slot_of[s][j], leaving)
            source_of[k][j] = found
            home = jnp.where(new_index == k * rows + slot_of[receiver][j], leaving, home)
    move_to = jnp.where(old_index == home, 1.0, 0.0).astype(BF16)

    for copy in one_copies:
        copy.wait()
    for k in range(n_ep):
        for j in range(moves):
            send2[k, j] = recv1[source_of[k][j], j]
    for copy in stream_copies:
        copy.wait()
    two_copies = [send(send2.at[k], recv2.at[k], two_sems, (k,), k) for k in range(1, n_ep)]
    recv2[0] = send2[0]

    gain_row = gain[...].reshape(1, width)
    known = streams[...].reshape(all_rows, width)
    wide = known.astype(F32)
    mean_square = jnp.sum(wide * wide, axis=1, keepdims=True) * (1.0 / width)
    tokens = (wide * lax.rsqrt(mean_square + EPSILON) * gain_row).astype(BF16)
    gate_part = jnp.dot(tokens, gate_w[...], preferred_element_type=F32)
    up_part = jnp.dot(tokens, up_w[...], preferred_element_type=F32)
    hidden[...] = ((up_part + 1.0) * gate_part * jax.nn.sigmoid(ALPHA * gate_part)).astype(BF16)
    moved = jnp.dot(move_to, hidden[...], preferred_element_type=F32).astype(BF16)
    loads[3].wait()
    expert_out = jnp.dot(moved, down_w[...], preferred_element_type=F32)
    for c in range(n_tp):
        ysend[c] = (
            expert_out[:, c * half : (c + 1) * half].astype(BF16).reshape(n_ep, rows, half)
        )
    y_copies = []
    for q in range(n_tp):
        core = lax.rem(tp + q, n_tp)
        for k in range(n_ep):
            if k or q:
                y_copies.append(send(ysend.at[core, k], yrecv.at[q, k], y_sems, (q, k), k, q))
    yrecv[0, 0] = ysend[tp, 0]

    row_index = lax.broadcasted_iota(jnp.int32, (rows, 1), 0)
    kept = row_index >= 0
    for j in range(moves):
        kept = kept & (row_index != slot_of[0][j])
    brought = jnp.dot(move_to[0:rows], known, preferred_element_type=F32)
    new_stream = jnp.where(kept, own_stream[...], brought)
    mean_square = jnp.sum(new_stream * new_stream, axis=1, keepdims=True) * (1.0 / width)
    normed = new_stream * lax.rsqrt(mean_square + EPSILON) * gain_row
    logits = lax.dot_general(
        router[...].astype(F32),
        normed,
        (((1,), (1,)), ((), ())),
        precision=lax.Precision.HIGHEST,
        preferred_element_type=F32,
    )
    expert_index = lax.broadcasted_iota(jnp.int32, logits.shape, 0)
    chosen = jnp.zeros(logits.shape, F32)
    for t in range(expert_ids.shape[0]):
        chosen = jnp.where(expert_index == expert_ids[t : t + 1, :], 1.0, chosen)
    best = jnp.max(jnp.where(chosen > 0.5, logits, -1e30), axis=0, keepdims=True)
    raised = jnp.where(chosen > 0.5, jnp.exp(logits - best), 0.0)
    gates = raised / jnp.sum(raised, axis=0, keepdims=True)
    slot_index = lax.broadcasted_iota(jnp.int32, (n_ep, n_ep), 1)
    owner = lax.broadcasted_iota(jnp.int32, (n_ep, n_ep), 0)
    order = jnp.where(wrap(ep - slot_index, n_ep) == owner, 1.0, 0.0)
    by_slot = lax.dot_general(
        gates,
        order,
        (((0,), (0,)), ((), ())),
        precision=lax.Precision.HIGHEST,
        preferred_element_type=F32,
    )
    result = new_stream[:, 0:half]
    for c in range(1, n_tp):
        result = jnp.where(tp == c, new_stream[:, c * half : (c + 1) * half], result)
    for copy in y_copies:
        copy.wait()
    for k in range(n_ep):
        gate = by_slot[:, k : k + 1]
        summed = yrecv[0, k].astype(F32)
        for q in range(1, n_tp):
            summed = summed + yrecv[q, k].astype(F32)
        result = result + gate * summed
    layer_out[...] = result.astype(BF16)

    for copy in two_copies:
        copy.wait()
    for k in range(n_ep):
        for j in range(moves):
            incoming[j, behind(k)] = recv2[k, j]
    store.wait()


def place_kernel(slots, filled, incoming, placed, row_sems, move_sems):
    rows, moves = filled.shape[0], incoming.shape[0]
    arrivals = [
        pltpu.make_async_copy(incoming.at[j], placed.at[slots[j]], move_sems.at[j])
        for j in range(moves)
    ]
    stays = []
    for r in range(rows):
        stay = slots[0] != r
        for j in range(1, moves):
            stay = stay & (slots[j] != r)
        stays.append((stay, pltpu.make_async_copy(filled.at[r], placed.at[r], row_sems.at[r])))
    for copy in arrivals:
        copy.start()
    for stay, copy in stays:
        pl.when(stay)(copy.start)
    for copy in arrivals:
        copy.wait()
    for stay, copy in stays:
        pl.when(stay)(copy.wait)


def per_device(
    n_ep,
    n_tp,
    residual,
    queries,
    new_kv,
    kv_cache,
    cache_len,
    move_slot,
    move_dest,
    sink_logits,
    out_weight,
    norm_gain,
    router_weight,
    expert_ids,
    gate_up,
    down_weight,
):
    rows, width = residual.shape
    _, _, kv, hd, length = kv_cache.shape
    moves = move_slot.shape[0]
    q_heads = sink_logits.shape[0]
    hidden_units = down_weight.shape[1]
    pieces = kv_cache.reshape(rows, 2 * kv, hd, length)
    piece = (moves, hd, length)
    half = width // n_tp
    smem = pl.BlockSpec(memory_space=pltpu.SMEM)
    vmem = pl.BlockSpec(memory_space=pltpu.VMEM)
    hbm = pl.BlockSpec(memory_space=pl.ANY)
    dma = pltpu.SemaphoreType.DMA
    layer_out, incoming, filled = pl.pallas_call(
        functools.partial(step_kernel, n_ep, n_tp),
        out_shape=(
            jax.ShapeDtypeStruct((rows, half), BF16),
            jax.ShapeDtypeStruct((moves, 2 * kv, hd, length), BF16),
            jax.ShapeDtypeStruct(pieces.shape, BF16),
        ),
        in_specs=[smem] * 4 + [vmem] * 6 + [hbm] * 4,
        out_specs=(vmem, vmem, hbm),
        scratch_shapes=[
            pltpu.VMEM((8, 128), jnp.int32),
            pltpu.VMEM((rows, q_heads, kv * hd), F32),
            pltpu.VMEM(pieces.shape, BF16),
            pltpu.VMEM((width, out_weight.shape[0]), BF16),
            pltpu.VMEM((width, 2, hidden_units), BF16),
            pltpu.VMEM((width, hidden_units), BF16),
            pltpu.VMEM((width, hidden_units), BF16),
            pltpu.VMEM((hidden_units, width), BF16),
            pltpu.VMEM((2 * kv,) + piece, BF16),
            pltpu.VMEM((n_ep,) + piece, BF16),
            pltpu.VMEM((n_ep,) + piece, BF16),
            pltpu.VMEM((n_ep,) + piece, BF16),
            pltpu.VMEM((n_ep, 8, 128), jnp.int32),
            pltpu.SMEM((n_ep, 8, 128), jnp.int32),
            pltpu.VMEM((rows, q_heads, kv * hd), F32),
            pltpu.VMEM((rows, q_heads * hd), BF16),
            pltpu.VMEM((rows, width), F32),
            pltpu.VMEM((n_tp, rows, width), F32),
            pltpu.VMEM((rows, width), F32),
            pltpu.VMEM((n_ep, rows, width), BF16),
            pltpu.VMEM((n_ep * rows, hidden_units), BF16),
            pltpu.VMEM((n_tp, n_ep, rows, half), BF16),
            pltpu.VMEM((n_tp, n_ep, rows, half), BF16),
            dma((4,)),
            dma((2, n_ep)),
            dma((2, n_ep)),
            dma((2, n_ep)),
            dma((2, n_tp)),
            dma((2, n_ep)),
            dma((2, n_tp, n_ep)),
            dma,
            dma,
        ],
        compiler_params=pltpu.CompilerParams(
            collective_id=0, has_side_effects=True, vmem_limit_bytes=58 * 1024 * 1024
        ),
    )(
        cache_len,
        move_slot,
        move_dest,
        sink_logits,
        queries,
        new_kv,
        residual,
        norm_gain,
        router_weight.T,
        expert_ids.T,
        pieces,
        out_weight.T,
        gate_up[0],
        down_weight[0],
    )
    cache_out = pl.pallas_call(
        place_kernel,
        out_shape=jax.ShapeDtypeStruct(pieces.shape, BF16),
        in_specs=[smem, hbm, hbm],
        out_specs=hbm,
        scratch_shapes=[dma((rows,)), dma((moves,))],
    )(move_slot, filled, incoming)
    cache_out = cache_out.reshape(kv_cache.shape)
    return layer_out, cache_out


def solution(mesh):
    n_ep, n_tp = mesh.shape["ep"], mesh.shape["tp"]

    def body(*arrays):
        kv_cache, gate_up = arrays[3], arrays[12]
        if 2 * kv_cache.shape[2] == n_ep and gate_up.shape[0] == 1 and n_tp == 2:
            return per_device(n_ep, n_tp, *arrays)
        return per_device_general(*arrays)

    in_specs = (
        P(("groups", "ep"), None),
        P(("groups", "ep"), "tp"),
        P(("groups", "ep"), None, "tp"),
        P(("groups", "ep"), None, "tp", None, None),
        P(("groups", "ep")),
        P(("groups", "ep")),
        P(("groups", "ep")),
        P("tp"),
        P("tp", None),
        P(),
        P(),
        P(("groups", "ep"), None),
        P("ep", None, None, "tp"),
        P("ep", "tp", None),
    )
    out_specs = (P(("groups", "ep"), "tp"), P(("groups", "ep"), None, "tp", None, None))
    return jax.shard_map(
        body, mesh=mesh, in_specs=in_specs, out_specs=out_specs, check_vma=False
    )
```
